32 devices in a mesh: groups: 2 (over x), gx: 4 (over y, core), gy: 4 (over z).
Axes of the slice: x: 2, y: 2, z: 4, core: 2. Of those that a mesh axis runs over, the one named last changes fastest.
Arguments:
- hidden_state: bfloat16 [512, 8192], P('groups', 'gx'), parts along dimension 0
- cache_row: int32 [512], P('groups'), parts along dimension 0, may hold values from 0 to 255, each once
- ctx_len: int32 [512], P('groups'), parts along dimension 0, may hold values from 2 to 192, as said below
- w_query: bfloat16 [8192, 8192], P('gx', 'gy'), may hold values from -0.0625 to 0.0625
- w_key: bfloat16 [8192, 1024], P('gx', 'gy'), may hold values from -0.0625 to 0.0625
- w_value: bfloat16 [8192, 1024], P('gx', 'gy'), may hold values from -0.0625 to 0.0625
- w_output: bfloat16 [8192, 8192], P('gy', 'gx'), may hold values from -0.5 to 0.5
- k_cache: bfloat16 [512, 192, 1024], P(('groups', 'gx', 'gy')), parts along dimension 0
- v_cache: bfloat16 [512, 192, 1024], P(('groups', 'gx', 'gy')), parts along dimension 0, may hold values from -6 to 6
Outputs:
- mixed: bfloat16 [512, 8192], P(('groups', 'gy'), 'gx'), parts along dimension 0
The draws below stay inside these ranges and needn't reach their ends.
There are 2 independent parts, one for each index of `groups`. The reference program is written for one: setup_inputs(seed, part) draws one part's arguments, and reference() takes and returns one part's arrays. A program takes and returns all parts, laid end to end along the dimension named above; an argument that names none is the same for every part. Nothing has to cross between parts.
Inputs may be any that keep to these rules, and one draw needn't show every extreme that they name: cache_row is a permutation: request r's cache lies in cache row cache_row[r], and every row holds one request. Slots 0 to ctx_len[r] - 1 of a request's cache row are valid; the new token sits at position ctx_len[r]. Some request has exactly 192.
All inputs are finite; a program needn't handle non-finite values.
Results may differ from the reference program's by a relative error of at most 0.012.
The reference program's roundings to bfloat16 on the way (of `query`, `key_new`, `value_new`, `query_rot`, `key_rot`, `probs` and `attn`) count: a program that leaves them out, or rounds other values in their place, can miss the bound.
Values may be sent and summed in bfloat16 or wider, within the bound.
A program may use at most 128 MiB of HBM per device.

```python
import math
import jax
import jax.numpy as jnp
from jax import lax

D = 8192
H = 64
KVH = 8
HD = 128
CTX = 192
REQ = 256


def draw_hidden_state(key, part):
    key = jax.random.fold_in(key, 11)
    first_key = jax.random.fold_in(key, 0)
    ramp = jnp.exp(jnp.linspace(jnp.log(0.3), jnp.log(3.0), D)).astype(jnp.float32)
    values = jnp.clip(jax.random.normal(first_key, (REQ, D)), -6.0, 6.0) * ramp[None, :]
    return values.astype(jnp.float32).astype(jnp.bfloat16)


def draw_ctx_len(key, part):
    key = jax.random.fold_in(key, 37)
    first_key, second_key, third_key = jax.random.split(key, 3)
    first = jax.random.randint(first_key, (REQ,), 0, CTX)
    second = jax.random.randint(second_key, (REQ,), 0, CTX)
    lengths = 2 + first * second // CTX
    chosen = jax.random.randint(third_key, (), 0, REQ)
    lengths = jnp.where(jnp.arange(REQ) == chosen, CTX, lengths)
    return jnp.minimum(lengths, CTX).astype(jnp.int32)


def draw_k_cache(key, part):
    key = jax.random.fold_in(key, 23)
    first_key = jax.random.fold_in(key, 0)
    base = jnp.clip(jax.random.normal(first_key, (REQ, CTX, KVH * HD)), -6.0, 6.0)
    values = base
    return values.astype(jnp.float32).astype(jnp.bfloat16)


def steps_of(stream_key, dims, pieces, smallest, top_value):
    gain = 1.0
    for dim, blocks in pieces:
        draws = jax.random.uniform(jax.random.fold_in(jax.random.fold_in(stream_key, 6), dim), (blocks,), jnp.float32, smallest / len(pieces), top_value / len(pieces))
        gain = gain * jnp.repeat(jnp.exp(draws), dims[dim] // blocks).reshape((-1,) + (1,) * (len(dims) - 1 - dim))
    return gain


def bell_draw(own_key, shape, spread, reach, pieces=(), kind=jnp.bfloat16):
    array = jax.random.normal(own_key, shape, jnp.float32) * spread
    if len(pieces) > 0:
        array = steps_of(own_key, shape, pieces, -0.22, 0.18) * array
    return jnp.clip(array, min=-reach, max=reach).astype(kind)


def setup_inputs(seed: int = 0, part: int = 0) -> dict:
    streams_of = jax.random.split(jax.random.key(seed), 10)
    part_splits = jax.random.split(jax.random.fold_in(streams_of[9], part), 10)
    return {
        "hidden_state": draw_hidden_state(jax.random.fold_in(jax.random.fold_in(streams_of[9], part), 71), part),
        "cache_row": jax.random.permutation(part_splits[1], REQ).astype(jnp.int32),
        "ctx_len": draw_ctx_len(jax.random.fold_in(jax.random.fold_in(streams_of[9], part), 71), part),
        "w_query": bell_draw(streams_of[3], (D, H * HD), D ** -0.5, 0.0625, ((0, 4), (1, 4))),
        "w_key": bell_draw(streams_of[4], (D, KVH * HD), D ** -0.5, 0.0625, ((0, 4), (1, 4))),
        "w_value": bell_draw(streams_of[5], (D, KVH * HD), D ** -0.5, 0.0625, ((0, 4), (1, 4))),
        "w_output": bell_draw(streams_of[6], (H * HD, D), HD ** -0.5, 0.5, ((0, 4), (1, 4))),
        "k_cache": draw_k_cache(jax.random.fold_in(jax.random.fold_in(streams_of[9], part), 71), part),
        "v_cache": bell_draw(part_splits[8], (REQ, CTX, KVH * HD), 1.0, 6.0, ((0, 16),)),
    }


EPS = 1e-05
THETA = 500000.0

def rotate(values, position):
    half = values.shape[-1] // 2
    index = jnp.arange(half, dtype=jnp.float32)
    freq = jnp.exp(index * (-2.0 * math.log(THETA) / values.shape[-1]))
    angle = position[:, None, None] * freq[None, None, :]
    cosine = jnp.cos(angle)
    sine = jnp.sin(angle)
    first = values[..., :half]
    second = values[..., half:]
    return jnp.concatenate([first * cosine - second * sine, second * cosine + first * sine], axis=-1)

def attend(query, key_new, value_new, key_cache, value_cache, lengths):
    count = query.shape[0]
    context = key_cache.shape[1]
    group = H // KVH
    scale = 1.0 / math.sqrt(HD)
    position = lengths.astype(jnp.float32)
    query_rot = rotate(query.astype(jnp.float32).reshape(count, H, HD), position).astype(jnp.bfloat16)
    query_rot = query_rot.reshape(count, KVH, group, HD).astype(jnp.float32)
    key_rot = rotate(key_new.astype(jnp.float32).reshape(count, KVH, HD), position).astype(jnp.bfloat16).astype(jnp.float32)
    keys = key_cache.reshape(count, context, KVH, HD).astype(jnp.float32)
    values = value_cache.reshape(count, context, KVH, HD).astype(jnp.float32)
    scores = jnp.einsum('rkgd,rckd->rkgc', query_rot, keys) * scale
    self_score = jnp.einsum('rkgd,rkd->rkg', query_rot, key_rot) * scale
    valid = (jnp.arange(context, dtype=jnp.int32)[None, :] < lengths[:, None])[:, None, None, :]
    highest = jnp.maximum(lax.optimization_barrier(jnp.max(jnp.where(valid, scores, -jnp.inf), axis=-1)), self_score)
    weights = jnp.where(valid, jnp.exp(scores - highest[..., None]), 0.0)
    self_weight = jnp.exp(self_score - highest)
    denominator = lax.optimization_barrier(jnp.sum(weights, axis=-1)) + self_weight
    probs = lax.optimization_barrier(weights.astype(jnp.bfloat16)).astype(jnp.float32)
    self_prob = lax.optimization_barrier(self_weight.astype(jnp.bfloat16)).astype(jnp.float32)
    value_self = value_new.reshape(count, KVH, HD).astype(jnp.float32)
    summed = jnp.einsum('rkgc,rckd->rkgd', probs, values) + self_prob[..., None] * value_self[:, :, None, :]
    return (summed / denominator[..., None]).astype(jnp.bfloat16).reshape(count, H * HD)

def reference(hidden_state, cache_row, ctx_len, w_query, w_key, w_value, w_output, k_cache, v_cache):
    squares = lax.optimization_barrier(jnp.sum(jnp.square(hidden_state.astype(jnp.float32)), axis=1))
    inv_rms = lax.rsqrt(squares / D + EPS)[:, None]
    query = (jnp.dot(hidden_state, w_query, preferred_element_type=jnp.float32) * inv_rms).astype(jnp.bfloat16)
    key_new = (jnp.dot(hidden_state, w_key, preferred_element_type=jnp.float32) * inv_rms).astype(jnp.bfloat16)
    value_new = (jnp.dot(hidden_state, w_value, preferred_element_type=jnp.float32) * inv_rms).astype(jnp.bfloat16)

    def one_request(request):
        row_index = lax.dynamic_slice_in_dim(cache_row, request, 1)[0]
        return attend(lax.dynamic_slice_in_dim(query, request, 1), lax.dynamic_slice_in_dim(key_new, request, 1), lax.dynamic_slice_in_dim(value_new, request, 1), lax.dynamic_slice_in_dim(k_cache, row_index, 1), lax.dynamic_slice_in_dim(v_cache, row_index, 1), lax.dynamic_slice_in_dim(ctx_len, request, 1))[0]
    attn = lax.map(one_request, jnp.arange(REQ, dtype=jnp.int32))
    return jnp.dot(attn, w_output, preferred_element_type=jnp.float32).astype(jnp.bfloat16)
```

```python
import functools
import math

import jax
import jax.numpy as jnp
from jax import lax
from jax.experimental import pallas as pl
from jax.experimental.pallas import tpu as pltpu
from jax.sharding import PartitionSpec as P

D = 8192
H = 64
KVH = 8
HD = 128
EPS = 1e-05
THETA = 500000.0
MESH = pl.DeviceIdType.MESH
F32 = jnp.float32
BF16 = jnp.bfloat16
NCH = 5
NOUT = 4
PAD = 16


def kernel(
    gxn, gyn,
    hidden, crow_lane, crow_col, cos2, sin2, bias,
    w_query, w_key, w_value, w_output, k_cache, v_cache,
    out,
    wbuf, wobuf, kbuf, vbuf, ordered, sq, own, xsend, xrecv, sqrecv, ysend, yrecv, mine,
    sqysend, sqyrecv, inv, fin, qrecv, qs, os, asend, gath, perm, fsend, frecv, facc,
    w_sem, wo_sem, kv_sem, xs, xr, ys, yr, qsem, qr, asem, ar, es, er, cs, cr, fs, fr,
):
    gx = lax.axis_index("gx")
    gy = lax.axis_index("gy")
    ny = gxn // 2
    y = gx // 2
    core = gx % 2
    partner = y * 2 + (1 - core)
    ctx = k_cache.shape[1]
    rl = k_cache.shape[0]
    blk = ordered.shape[1]
    requests = blk * gxn
    hl = H // gyn
    kvl = KVH // gyn
    group = H // KVH
    cw = wbuf.shape[2]
    half = cw // 2
    ow = wobuf.shape[2]

    def ypeer(j):
        return lax.rem(y + j, ny)

    def zpeer(k):
        return lax.rem(gy + k, gyn)

    w_copies = [
        [pltpu.make_async_copy(w_query.at[:, pl.ds(c * cw, cw)], wbuf.at[c], w_sem.at[c])]
        for c in range(NCH - 1)
    ]
    w_copies.append([
        pltpu.make_async_copy(w_key, wbuf.at[NCH - 1, :, pl.ds(0, half)], w_sem.at[NCH - 1]),
        pltpu.make_async_copy(w_value, wbuf.at[NCH - 1, :, pl.ds(half, half)], w_sem.at[NCH]),
    ])
    order = [NCH - 1] + list(range(NCH - 1))
    for c in order:
        for copy in w_copies[c]:
            copy.start()
    kv_copies = [
        pltpu.make_async_copy(k_cache, kbuf.at[:, pl.ds(0, ctx), :], kv_sem.at[0]),
        pltpu.make_async_copy(v_cache, vbuf.at[:, pl.ds(0, ctx), :], kv_sem.at[1]),
    ]
    wo_copies = [
        pltpu.make_async_copy(w_output.at[:, pl.ds(n * ow, ow)], wobuf.at[n], wo_sem.at[n])
        for n in range(NOUT)
    ]

    barrier = pltpu.get_barrier_semaphore()
    pl.semaphore_signal(barrier, inc=1, device_id={"gx": partner}, device_id_type=MESH)
    for j in range(1, ny):
        pl.semaphore_signal(
            barrier, inc=1, device_id={"gx": ypeer(j) * 2 + core}, device_id_type=MESH
        )
    for k in range(1, gyn):
        pl.semaphore_signal(barrier, inc=1, device_id={"gy": zpeer(k)}, device_id_type=MESH)

    def reorder(b, carry):
        parity = jnp.where(b < ny, 1 - core, core)
        source = lax.rem(y + lax.rem(b, ny), ny) * 2 + parity
        wanted = lax.broadcasted_iota(jnp.int32, (blk, requests), 0) + source * blk
        chosen = jnp.where(crow_lane[...] == wanted, 1.0, 0.0).astype(BF16)
        rows = jnp.dot(chosen, hidden[...], preferred_element_type=F32)
        ordered[b] = rows.astype(BF16)
        sq[b] = jnp.broadcast_to(jnp.sum(rows * rows, axis=1, keepdims=True), (blk, HD))
        return carry

    lax.fori_loop(0, gxn, reorder, 0)
    pl.semaphore_wait(barrier, 1 + (ny - 1) + (gyn - 1))

    def remote(src, dst, send, recv, **where):
        return pltpu.make_async_remote_copy(
            src_ref=src, dst_ref=dst, send_sem=send, recv_sem=recv,
            device_id=where, device_id_type=MESH,
        )

    def x_copy(c):
        return remote(xsend.at[c], xrecv.at[c], xs.at[c], xr.at[c], gx=partner)

    def y_copy(c, j):
        return remote(
            ysend.at[c, j], yrecv.at[c, j], ys.at[c, j], yr.at[c, j], gx=ypeer(j) * 2 + core
        )

    sq_x = remote(sq.at[pl.ds(0, ny)], sqrecv, xs.at[NCH], xr.at[NCH], gx=partner)

    def sq_y(j):
        return remote(
            sqysend.at[j], sqyrecv.at[j], ys.at[NCH, j], yr.at[NCH, j], gx=ypeer(j) * 2 + core
        )

    def q_copy(c, k):
        peer = zpeer(k)
        return remote(
            fin.at[c, peer], qrecv.at[gy, c], qsem.at[c, k], qr.at[gy, c], gy=peer
        )

    def stage1(c):
        for copy in w_copies[c]:
            copy.wait()
        rows = ordered[...].reshape(requests, ordered.shape[2])
        part = jnp.dot(rows, wbuf[c], preferred_element_type=F32)
        xsend[c] = part[: requests // 2].astype(BF16)
        x_copy(c).start()
        own[c] = part[requests // 2 :]

    def stage2(c):
        x_copy(c).wait_recv()
        for j in range(1, ny):
            rows = pl.ds(j * blk, blk)
            ysend[c, j] = (own[c, rows, :] + xrecv[c, rows, :].astype(F32)).astype(BF16)
            y_copy(c, j).start()
        rows = pl.ds(0, blk)
        mine[c] = own[c, rows, :] + xrecv[c, rows, :].astype(F32)

    def stage3(c):
        total = mine[c]
        for j in range(1, ny):
            y_copy(c, j).wait_recv()
            total = total + yrecv[c, j].astype(F32)
        scaled = (total * inv[...]).astype(BF16)
        for k in range(gyn):
            fin[c, k] = scaled[k * rl : (k + 1) * rl]
        for k in range(1, gyn):
            q_copy(c, k).start()
        qrecv[gy, c] = fin[c, gy]

    sq_x.start()
    for step in range(NCH + 2):
        if step < NCH:
            stage1(order[step])
        if step == 1:
            for copy in kv_copies:
                copy.start()
            sq_x.wait_recv()
            for j in range(1, ny):
                sqysend[j] = sq[ny + j] + sqrecv[j]
                sq_y(j).start()
        if 1 <= step <= NCH:
            stage2(order[step - 1])
        if step == 2:
            total = sq[ny] + sqrecv[0]
            for j in range(1, ny):
                sq_y(j).wait_recv()
                total = total + sqyrecv[j]
            inv[...] = lax.rsqrt(total[:, :1] / D + EPS)
        if step >= 2:
            stage3(order[step - 2])
    for copy in wo_copies:
        copy.start()
    for copy in kv_copies:
        copy.wait()

    cosine = cos2[...]
    sine = sin2[...]
    scale = 1.0 / math.sqrt(HD)
    first_row = lax.broadcasted_iota(jnp.int32, (PAD, HD), 0) == 0
    head = lax.broadcasted_iota(jnp.int32, (hl, HD), 0) // group

    def turned(values):
        values = values.astype(F32)
        return values * cosine + pltpu.roll(values, HD // 2, 1) * sine

    def a_copy(k):
        peer = zpeer(k)
        return remote(asend.at[peer], gath.at[gx, gy], asem.at[k], ar.at[gy], gy=peer)

    def attention(k, carry):
        source = zpeer(k)

        @pl.when(k > 0)
        def _():
            for c in order:
                remote(
                    fin.at[c, source], qrecv.at[source, c], qsem.at[c, k], qr.at[source, c],
                    gy=source,
                ).wait_recv()

        for h in range(hl):
            at = h * HD
            q = qrecv[source, at // cw, :, at % cw : at % cw + HD]
            qs[:, h, :] = turned(q).astype(BF16).astype(F32)
        for g in range(kvl):
            key = turned(qrecv[source, NCH - 1, :, g * HD : (g + 1) * HD])
            value = qrecv[source, NCH - 1, :, half + g * HD : half + (g + 1) * HD].astype(F32)
            columns = pl.ds(pl.multiple_of((source * kvl + g) * HD, HD), HD)
            for r in range(rl):
                kbuf[r, pl.ds(ctx, PAD), columns] = jnp.where(
                    first_row, key[r : r + 1], 0.0
                ).astype(BF16)
                vbuf[r, pl.ds(ctx, PAD), columns] = jnp.where(
                    first_row, value[r : r + 1], 0.0
                ).astype(BF16)
        columns = pl.ds(pl.multiple_of(source * kvl * HD, kvl * HD), kvl * HD)
        scores = []
        for r in range(rl):
            q = qs[r]
            wide = jnp.concatenate(
                [jnp.where(head == g, q, 0.0) for g in range(kvl)], axis=1
            ).astype(BF16)
            scores.append(
                lax.dot_general(
                    wide, kbuf[r, :, columns], (((1,), (1,)), ((), ())),
                    preferred_element_type=F32,
                ) * scale + bias[r : r + 1]
            )
        for r in range(rl):
            highest = jnp.max(scores[r], axis=1, keepdims=True)
            weights = jnp.exp(scores[r] - highest)
            denominator = jnp.sum(weights, axis=1, keepdims=True)
            wide = jnp.dot(
                weights.astype(BF16), vbuf[r, :, columns], preferred_element_type=F32
            )
            picked = wide[:, :HD]
            for g in range(1, kvl):
                picked = jnp.where(head == g, wide[:, g * HD : (g + 1) * HD], picked)
            os[r] = picked / denominator
        for h in range(hl):
            asend[source, :, h * HD : (h + 1) * HD] = os[:, h, :].astype(BF16)

        @pl.when(k > 0)
        def _():
            a_copy(k).start()

        @pl.when(k == 0)
        def _():
            gath[gx, gy] = asend[gy]

        return carry

    lax.fori_loop(0, gyn, attention, 0)

    def e_copy(row, piece, j):
        return remote(
            gath.at[row, piece], gath.at[row, piece], es.at[j, piece], er.at[row // 2, piece],
            gx=ypeer(j) * 2 + core,
        )

    def c_copy(row, piece):
        return remote(
            gath.at[row, piece], gath.at[row, piece], cs.at[row // 2, piece],
            cr.at[row // 2, piece], gx=partner,
        )

    for k in range(gyn):
        piece = zpeer(k)
        if k > 0:
            remote(
                asend.at[piece], gath.at[gx, piece], asem.at[k], ar.at[piece], gy=piece
            ).wait_recv()
        for j in range(1, ny):
            e_copy(gx, piece, j).start()
        c_copy(gx, piece).start()
    for k in range(gyn):
        piece = zpeer(k)
        for j in range(1, ny):
            row = ypeer(j) * 2 + core
            e_copy(row, piece, j).wait_recv()
            c_copy(row, piece).start()
    for k in range(gyn):
        piece = zpeer(k)
        for j in range(ny):
            c_copy(ypeer(j) * 2 + 1 - core, piece).wait_recv()

    zblk = perm.shape[1]

    def permute(k, carry):
        wanted = crow_col[zpeer(k)]
        lanes = lax.broadcasted_iota(jnp.int32, (zblk, requests), 1)
        chosen = jnp.where(wanted == lanes, 1.0, 0.0).astype(BF16)
        rows = gath[...].reshape(requests, hl * HD)
        perm[k] = jnp.dot(chosen, rows, preferred_element_type=F32).astype(BF16)
        return carry

    lax.fori_loop(0, gyn, permute, 0)

    def f_copy(n, k):
        return remote(fsend.at[n, k], frecv.at[n, k], fs.at[n, k], fr.at[n, k], gy=zpeer(k))

    for n in range(NOUT):
        wo_copies[n].wait()
        rows = perm[...].reshape(requests, hl * HD)
        part = jnp.dot(rows, wobuf[n], preferred_element_type=F32)
        for k in range(1, gyn):
            fsend[n, k] = part[k * zblk : (k + 1) * zblk].astype(BF16)
            f_copy(n, k).start()
        facc[n] = part[:zblk]
    for n in range(NOUT):
        total = facc[n]
        for k in range(1, gyn):
            f_copy(n, k).wait_recv()
            total = total + frecv[n, k].astype(F32)
        out[:, n * ow : (n + 1) * ow] = total.astype(BF16)

    sq_x.wait_send()
    for j in range(1, ny):
        sq_y(j).wait_send()
    for c in range(NCH):
        x_copy(c).wait_send()
        for j in range(1, ny):
            y_copy(c, j).wait_send()
        for k in range(1, gyn):
            q_copy(c, k).wait_send()
    for k in range(1, gyn):
        a_copy(k).wait_send()
    for k in range(gyn):
        piece = zpeer(k)
        for j in range(1, ny):
            e_copy(gx, piece, j).wait_send()
        for j in range(ny):
            c_copy(ypeer(j) * 2 + core, piece).wait_send()
    for n in range(NOUT):
        for k in range(1, gyn):
            f_copy(n, k).wait_send()


def body(gxn, gyn, hidden, cache_row, ctx_len, w_query, w_key, w_value, w_output, k_cache, v_cache):
    requests = cache_row.shape[0]
    rl, ctx, width = k_cache.shape
    ny = gxn // 2
    blk = requests // gxn
    zblk = requests // gyn
    dl = hidden.shape[1]
    hl = H // gyn
    cols = w_query.shape[1] + w_key.shape[1] + w_value.shape[1]
    cw = cols // NCH
    outw = w_output.shape[1]
    ow = outw // NOUT

    first = (lax.axis_index("gx") * gyn + lax.axis_index("gy")) * rl
    rows = first + jnp.arange(rl, dtype=jnp.int32)
    lengths = jnp.sum(
        jnp.where(cache_row[None, :] == rows[:, None], ctx_len[None, :], 0), axis=1
    )
    freq = jnp.exp(jnp.arange(HD // 2, dtype=F32) * (-2.0 * math.log(THETA) / HD))
    angle = lengths.astype(F32)[:, None] * freq[None, :]
    cosine = jnp.cos(angle)
    sine = jnp.sin(angle)
    cos2 = jnp.concatenate([cosine, cosine], axis=1)
    sin2 = jnp.concatenate([-sine, sine], axis=1)
    slot = jnp.arange(ctx + PAD, dtype=jnp.int32)[None, :]
    bias = jnp.where((slot < lengths[:, None]) & (slot < ctx) | (slot == ctx), 0.0, -jnp.inf)

    vm = pl.BlockSpec(memory_space=pltpu.VMEM)
    hbm = pl.BlockSpec(memory_space=pl.ANY)
    dma = pltpu.SemaphoreType.DMA
    V = pltpu.VMEM
    return pl.pallas_call(
        functools.partial(kernel, gxn, gyn),
        out_shape=jax.ShapeDtypeStruct((zblk, outw), BF16),
        in_specs=[vm] * 6 + [hbm] * 6,
        out_specs=vm,
        scratch_shapes=[
            V((NCH, dl, cw), BF16),
            V((NOUT, hl * HD, ow), BF16),
            V((rl, ctx + PAD, width), BF16),
            V((rl, ctx + PAD, width), BF16),
            V((gxn, blk, dl), BF16),
            V((gxn, blk, HD), F32),
            V((NCH, requests // 2, cw), F32),
            V((NCH, requests // 2, cw), BF16),
            V((NCH, requests // 2, cw), BF16),
            V((ny, blk, HD), F32),
            V((NCH, ny, blk, cw), BF16),
            V((NCH, ny, blk, cw), BF16),
            V((NCH, blk, cw), F32),
            V((ny, blk, HD), F32),
            V((ny, blk, HD), F32),
            V((blk, 1), F32),
            V((NCH, gyn, rl, cw), BF16),
            V((gyn, NCH, rl, cw), BF16),
            V((rl, hl, HD), F32),
            V((rl, hl, HD), F32),
            V((gyn, rl, hl * HD), BF16),
            V((gxn, gyn, rl, hl * HD), BF16),
            V((gyn, zblk, hl * HD), BF16),
            V((NOUT, gyn, zblk, ow), BF16),
            V((NOUT, gyn, zblk, ow), BF16),
            V((NOUT, zblk, ow), F32),
            dma((NCH + 1,)), dma((NOUT,)), dma((2,)),
            dma((NCH + 1,)), dma((NCH + 1,)),
            dma((NCH + 1, ny)), dma((NCH + 1, ny)),
            dma((NCH, gyn)), dma((gyn, NCH)),
            dma((gyn,)), dma((gyn,)),
            dma((ny, gyn)), dma((ny, gyn)),
            dma((ny, gyn)), dma((ny, gyn)),
            dma((NOUT, gyn)), dma((NOUT, gyn)),
        ],
        compiler_params=pltpu.CompilerParams(
            collective_id=0, has_side_effects=True, vmem_limit_bytes=60 * 1024 * 1024
        ),
        cost_estimate=pl.CostEstimate(
            flops=2 * requests * dl * cols, bytes_accessed=2 * dl * cols, transcendentals=0
        ),
    )(
        hidden, cache_row[None, :], cache_row.reshape(gyn, zblk, 1), cos2, sin2, bias,
        w_query, w_key, w_value, w_output, k_cache, v_cache,
    )


def solution(mesh):
    placed = (
        P("groups", "gx"),
        P("groups"),
        P("groups"),
        P("gx", "gy"),
        P("gx", "gy"),
        P("gx", "gy"),
        P("gy", "gx"),
        P(("groups", "gx", "gy"), None, None),
        P(("groups", "gx", "gy"), None, None),
    )
    return jax.shard_map(
        functools.partial(body, mesh.shape["gx"], mesh.shape["gy"]),
        mesh=mesh, in_specs=placed, out_specs=P(("groups", "gy"), "gx"), check_vma=False,
    )
```

```python
import functools
import math

import jax
import jax.numpy as jnp
from jax import lax
from jax.experimental import pallas as pl
from jax.experimental.pallas import tpu as pltpu
from jax.sharding import PartitionSpec as P

D = 8192
H = 64
KVH = 8
HD = 128
EPS = 1e-05
THETA = 500000.0
MESH = pl.DeviceIdType.MESH
F32 = jnp.float32
BF16 = jnp.bfloat16
NCH = 5
NOUT = 4
AHEAD = 2
PAD = 16


def kernel(
    gxn, gyn,
    hidden, crow, clen,
    w_query, w_key, w_value, w_output, k_cache, v_cache,
    out,
    wbuf, wobuf, kbuf, vbuf, ordered, sq, own, xsend, xrecv, sqrecv, ysend, yrecv,
    sqysend, sqyrecv, inv, cos2, sin2, bias, fin, qrecv, qs, os, asend, gath, row_of, perm,
    fsend, frecv, mrecv, facc, fkeep,
    w_sem, wo_sem, kv_sem, xs, xr, ys, yr, qsem, qr, asem, ar, es, er, cs, cr, fs, fr, ms,
):
    gx = lax.axis_index("gx")
    gy = lax.axis_index("gy")
    ny = gxn // 2
    y = gx // 2
    core = gx % 2
    partner = y * 2 + (1 - core)
    ctx = k_cache.shape[1]
    rl = k_cache.shape[0]
    blk = ordered.shape[1]
    requests = blk * gxn
    hl = H // gyn
    kvl = KVH // gyn
    group = H // KVH
    cw = wbuf.shape[2]
    half = cw // 2
    ow = wobuf.shape[2]

    def ypeer(j):
        return lax.rem(y + j, ny)

    def zpeer(k):
        return lax.rem(gy + k, gyn)

    w_copies = [
        [pltpu.make_async_copy(w_query.at[:, pl.ds(c * cw, cw)], wbuf.at[c], w_sem.at[c])]
        for c in range(NCH - 1)
    ]
    w_copies.append([
        pltpu.make_async_copy(w_key, wbuf.at[NCH - 1, :, pl.ds(0, half)], w_sem.at[NCH - 1]),
        pltpu.make_async_copy(w_value, wbuf.at[NCH - 1, :, pl.ds(half, half)], w_sem.at[NCH]),
    ])
    order = [NCH - 1] + list(range(NCH - 1))
    for c in order:
        for copy in w_copies[c]:
            copy.start()
    kv_copies = [
        pltpu.make_async_copy(k_cache, kbuf.at[:, pl.ds(0, ctx), :], kv_sem.at[0]),
        pltpu.make_async_copy(v_cache, vbuf.at[:, pl.ds(0, ctx), :], kv_sem.at[1]),
    ]
    wo_copies = [
        pltpu.make_async_copy(w_output.at[:, pl.ds(n * ow, ow)], wobuf.at[n], wo_sem.at[n])
        for n in range(NOUT)
    ]

    barrier = pltpu.get_barrier_semaphore()
    pl.semaphore_signal(barrier, inc=1, device_id={"gx": partner}, device_id_type=MESH)
    for j in range(1, ny):
        pl.semaphore_signal(
            barrier, inc=1, device_id={"gx": ypeer(j) * 2 + core}, device_id_type=MESH
        )
    for k in range(1, gyn):
        pl.semaphore_signal(barrier, inc=1, device_id={"gy": zpeer(k)}, device_id_type=MESH)

    def reorder(b, carry):
        parity = jnp.where(b < ny, 1 - core, core)
        source = lax.rem(y + lax.rem(b, ny), ny) * 2 + parity
        wanted = lax.broadcasted_iota(jnp.int32, (blk, requests), 0) + source * blk
        chosen = jnp.where(crow[...] == wanted, 1.0, 0.0).astype(BF16)
        rows = jnp.dot(chosen, hidden[...], preferred_element_type=F32)
        ordered[b] = rows.astype(BF16)
        sq[b] = jnp.broadcast_to(jnp.sum(rows * rows, axis=1, keepdims=True), (blk, HD))
        return carry

    for copy in kv_copies + wo_copies:
        copy.start()
    lax.fori_loop(0, gxn, reorder, 0)

    def remote(src, dst, send, recv, **where):
        return pltpu.make_async_remote_copy(
            src_ref=src, dst_ref=dst, send_sem=send, recv_sem=recv,
            device_id=where, device_id_type=MESH,
        )

    def x_copy(c):
        return remote(xsend.at[c], xrecv.at[c], xs.at[c], xr.at[c], gx=partner)

    def y_copy(c, j):
        return remote(
            ysend.at[c, j - 1], yrecv.at[c, j - 1], ys.at[c, j], yr.at[c, j], gx=ypeer(j) * 2 + core
        )

    sq_x = remote(sq.at[pl.ds(0, ny)], sqrecv, xs.at[NCH], xr.at[NCH], gx=partner)

    def sq_y(j):
        return remote(
            sqysend.at[j], sqyrecv.at[j], ys.at[NCH, j], yr.at[NCH, j], gx=ypeer(j) * 2 + core
        )

    def q_copy(c, k):
        peer = zpeer(k)
        return remote(
            fin.at[c, peer], qrecv.at[gy, c], qsem.at[c, k], qr.at[gy, c], gy=peer
        )

    def product(c):
        for copy in w_copies[c]:
            copy.wait()
        rows = ordered[...].reshape(requests, ordered.shape[2])
        part = jnp.dot(rows, wbuf[c], preferred_element_type=F32)
        xsend[c] = part[: requests // 2].astype(BF16)
        own[c] = part[requests // 2 :]

    def stage2(c):
        x_copy(c).wait_recv()
        for j in range(1, ny):
            rows = pl.ds(j * blk, blk)
            ysend[c, j - 1] = (own[c, rows, :] + xrecv[c, rows, :].astype(F32)).astype(BF16)
            y_copy(c, j).start()
        rows = pl.ds(0, blk)
        own[c, rows, :] = own[c, rows, :] + xrecv[c, rows, :].astype(F32)

    def stage3(c):
        total = own[c, pl.ds(0, blk), :]
        for j in range(1, ny):
            y_copy(c, j).wait_recv()
            total = total + yrecv[c, j - 1].astype(F32)
        scaled = (total * inv[...]).astype(BF16)
        for k in range(gyn):
            fin[c, k] = scaled[k * rl : (k + 1) * rl]
        for k in range(1, gyn):
            q_copy(c, k).start()
        qrecv[gy, c] = fin[c, gy]

    for c in order[:AHEAD]:
        product(c)
    first_row = (gx * gyn + gy) * rl
    wanted = lax.broadcasted_iota(jnp.int32, (rl, requests), 0) + first_row
    lengths = jnp.sum(
        jnp.where(crow[...] == wanted, clen[...].astype(F32), 0.0), axis=1, keepdims=True
    )
    lane = lax.broadcasted_iota(jnp.int32, (1, HD), 1)
    pair = lax.rem(lane, HD // 2).astype(F32)
    angle = lengths * jnp.exp(pair * (-2.0 * math.log(THETA) / HD))
    cos2[...] = jnp.cos(angle)
    sine = jnp.sin(angle)
    sin2[...] = jnp.where(lane < HD // 2, -sine, sine)
    slot = lax.broadcasted_iota(jnp.int32, (rl, ctx + PAD), 1)
    bias[...] = jnp.where(
        (slot == ctx) | ((slot < ctx) & (slot.astype(F32) < lengths)), 0.0, -jnp.inf
    )

    def select(b, carry):
        at = pl.ds(pl.multiple_of(b * HD, HD), HD)
        row_of[at, :] = jnp.broadcast_to(crow[:, at].astype(F32), (HD, HD)).T
        return carry

    lax.fori_loop(0, requests // HD, select, 0)
    pl.semaphore_wait(barrier, 1 + (ny - 1) + (gyn - 1))

    sq_x.start()
    for c in order[:AHEAD]:
        x_copy(c).start()
    for step in range(NCH + 2):
        if AHEAD <= step < NCH:
            product(order[step])
            x_copy(order[step]).start()
        if step == 1:
            sq_x.wait_recv()
            for j in range(1, ny):
                sqysend[j] = sq[ny + j] + sqrecv[j]
                sq_y(j).start()
        if 1 <= step <= NCH:
            stage2(order[step - 1])
        if step == 2:
            total = sq[ny] + sqrecv[0]
            for j in range(1, ny):
                sq_y(j).wait_recv()
                total = total + sqyrecv[j]
            inv[...] = lax.rsqrt(total[:, :1] / D + EPS)
        if step >= 2:
            stage3(order[step - 2])
    for copy in kv_copies:
        copy.wait()

    cosine = cos2[...]
    turn = sin2[...]
    scale = 1.0 / math.sqrt(HD)
    top = lax.broadcasted_iota(jnp.int32, (PAD, HD), 0) == 0
    head = lax.broadcasted_iota(jnp.int32, (hl, HD), 0) // group

    def turned(values):
        values = values.astype(F32)
        return values * cosine + pltpu.roll(values, HD // 2, 1) * turn

    def a_copy(k):
        peer = zpeer(k)
        return remote(asend.at[peer], gath.at[gx, gy], asem.at[k], ar.at[gy], gy=peer)

    def e_copy(row, piece, j):
        return remote(
            gath.at[row, piece], gath.at[row, piece], es.at[j, piece], er.at[row // 2, piece],
            gx=ypeer(j) * 2 + core,
        )

    def c_copy(row, piece):
        return remote(
            gath.at[row, piece], gath.at[row, piece], cs.at[row // 2, piece],
            cr.at[row // 2, piece], gx=partner,
        )

    def attention(k, carry):
        source = zpeer(k)

        @pl.when(k > 0)
        def _():
            for c in order:
                remote(
                    fin.at[c, source], qrecv.at[source, c], qsem.at[c, k], qr.at[source, c],
                    gy=source,
                ).wait_recv()

        for h in range(hl):
            at = h * HD
            q = qrecv[source, at // cw, :, at % cw : at % cw + HD]
            qs[:, h, :] = turned(q).astype(BF16).astype(F32)
        for g in range(kvl):
            key = turned(qrecv[source, NCH - 1, :, g * HD : (g + 1) * HD])
            value = qrecv[source, NCH - 1, :, half + g * HD : half + (g + 1) * HD].astype(F32)
            columns = pl.ds(pl.multiple_of((source * kvl + g) * HD, HD), HD)
            for r in range(rl):
                kbuf[r, pl.ds(ctx, PAD), columns] = jnp.where(
                    top, key[r : r + 1], 0.0
                ).astype(BF16)
                vbuf[r, pl.ds(ctx, PAD), columns] = jnp.where(
                    top, value[r : r + 1], 0.0
                ).astype(BF16)
        columns = pl.ds(pl.multiple_of(source * kvl * HD, kvl * HD), kvl * HD)
        scores = []
        for r in range(rl):
            q = qs[r]
            wide = jnp.concatenate(
                [jnp.where(head == g, q, 0.0) for g in range(kvl)], axis=1
            ).astype(BF16)
            scores.append(
                lax.dot_general(
                    wide, kbuf[r, :, columns], (((1,), (1,)), ((), ())),
                    preferred_element_type=F32,
                ) * scale + bias[pl.ds(r, 1), :]
            )
        for r in range(rl):
            highest = jnp.max(scores[r], axis=1, keepdims=True)
            weights = jnp.exp(scores[r] - highest)
            denominator = jnp.sum(weights, axis=1, keepdims=True)
            wide = jnp.dot(
                weights.astype(BF16), vbuf[r, :, columns], preferred_element_type=F32
            )
            picked = wide[:, :HD]
            for g in range(1, kvl):
                picked = jnp.where(head == g, wide[:, g * HD : (g + 1) * HD], picked)
            os[r] = picked / denominator
        for h in range(hl):
            asend[source, :, h * HD : (h + 1) * HD] = os[:, h, :].astype(BF16)

        @pl.when(k > 0)
        def _():
            a_copy(k).start()

        @pl.when(k == 0)
        def _():
            gath[gx, gy] = asend[gy]
            for j in range(1, ny):
                e_copy(gx, gy, j).start()
            c_copy(gx, gy).start()

        return carry

    lax.fori_loop(0, gyn, attention, 0)

    def zback(k):
        return lax.rem(gy - k + gyn, gyn)

    for k in range(1, gyn):
        piece = zback(k)
        remote(
            asend.at[piece], gath.at[gx, piece], asem.at[k], ar.at[piece], gy=piece
        ).wait_recv()
        for j in range(1, ny):
            e_copy(gx, piece, j).start()
        c_copy(gx, piece).start()
    for k in range(gyn):
        piece = zback(k)
        for j in range(1, ny):
            row = ypeer(j) * 2 + core
            e_copy(row, piece, j).wait_recv()
            c_copy(row, piece).start()
    for k in range(gyn):
        piece = zback(k)
        for j in range(ny):
            c_copy(ypeer(j) * 2 + 1 - core, piece).wait_recv()

    zblk = perm.shape[1]
    nh = gyn // 2
    side = gy // nh
    place = lax.rem(gy, nh)
    middle = jnp.where(side == 0, nh - 1 - place, place)

    def at_place(which, m):
        return jnp.where(which == 0, nh - 1 - m, nh + m)

    def target(t):
        if t < nh:
            return at_place(side, lax.rem(middle + t, nh))
        return at_place(1 - side, t - nh)

    for t in range(gyn):
        rows = pl.ds(pl.multiple_of(target(t) * zblk, zblk), zblk)
        lanes = lax.broadcasted_iota(jnp.int32, (zblk, requests), 1).astype(F32)
        chosen = jnp.where(row_of[rows, :1] == lanes, 1.0, 0.0).astype(BF16)
        perm[t] = jnp.dot(
            chosen, gath[...].reshape(requests, hl * HD), preferred_element_type=F32
        ).astype(BF16)

    def f_copy(n, t):
        if t < nh:
            return remote(
                fsend.at[n, t - 1], frecv.at[n, t], fs.at[n, t], fr.at[n, t], gy=target(t)
            )
        return remote(fsend.at[n, t - 1], frecv.at[n, 0], fs.at[n, t], fr.at[n, 0], gy=target(t))

    def m_copy(n, u, m):
        return remote(
            fsend.at[n, nh + u - 1], mrecv.at[n, u, m - 1], fs.at[n, nh + u], ms.at[n, u, m - 1],
            gy=at_place(side, 0),
        )

    def merge(n):
        @pl.when(middle == 0)
        def _():
            for u in range(nh):
                total = fkeep[n, u]
                for m in range(1, nh):
                    m_copy(n, u, m).wait_recv()
                    total = total + mrecv[n, u, m - 1].astype(F32)
                fsend[n, nh + u - 1] = total.astype(BF16)
                f_copy(n, nh + u).start()

    for n in range(NOUT):
        wo_copies[n].wait()
        rows = perm[...].reshape(requests, hl * HD)
        part = jnp.dot(rows, wobuf[n], preferred_element_type=F32)
        facc[n] = part[:zblk]
        for u in range(nh):
            fkeep[n, u] = part[(nh + u) * zblk : (nh + u + 1) * zblk]

        @pl.when(middle > 0)
        def _():
            for u in range(nh):
                fsend[n, nh + u - 1] = fkeep[n, u].astype(BF16)
                m_copy(n, u, middle).start()

        for t in range(1, nh):
            fsend[n, t - 1] = part[t * zblk : (t + 1) * zblk].astype(BF16)
            f_copy(n, t).start()
        if n > 0:
            merge(n - 1)
    merge(NOUT - 1)
    for n in range(NOUT):
        total = facc[n]
        for t in range(nh):
            f_copy(n, t if t > 0 else nh).wait_recv()
            total = total + frecv[n, t].astype(F32)
        out[:, n * ow : (n + 1) * ow] = total.astype(BF16)

    sq_x.wait_send()
    for j in range(1, ny):
        sq_y(j).wait_send()
    for c in range(NCH):
        x_copy(c).wait_send()
        for j in range(1, ny):
            y_copy(c, j).wait_send()
        for k in range(1, gyn):
            q_copy(c, k).wait_send()
    for k in range(1, gyn):
        a_copy(k).wait_send()
    for k in range(gyn):
        piece = zpeer(k)
        for j in range(1, ny):
            e_copy(gx, piece, j).wait_send()
        for j in range(ny):
            c_copy(ypeer(j) * 2 + core, piece).wait_send()
    for n in range(NOUT):
        for t in range(1, gyn):
            f_copy(n, t).wait_send()


def body(gxn, gyn, hidden, cache_row, ctx_len, w_query, w_key, w_value, w_output, k_cache, v_cache):
    requests = cache_row.shape[0]
    rl, ctx, width = k_cache.shape
    ny = gxn // 2
    blk = requests // gxn
    zblk = requests // gyn
    dl = hidden.shape[1]
    hl = H // gyn
    cols = w_query.shape[1] + w_key.shape[1] + w_value.shape[1]
    cw = cols // NCH
    outw = w_output.shape[1]
    ow = outw // NOUT

    vm = pl.BlockSpec(memory_space=pltpu.VMEM)
    hbm = pl.BlockSpec(memory_space=pl.ANY)
    dma = pltpu.SemaphoreType.DMA
    V = pltpu.VMEM
    return pl.pallas_call(
        functools.partial(kernel, gxn, gyn),
        out_shape=jax.ShapeDtypeStruct((zblk, outw), BF16),
        in_specs=[vm] * 3 + [hbm] * 6,
        out_specs=vm,
        scratch_shapes=[
            V((NCH, dl, cw), BF16),
            V((NOUT, hl * HD, ow), BF16),
            V((rl, ctx + PAD, width), BF16),
            V((rl, ctx + PAD, width), BF16),
            V((gxn, blk, dl), BF16),
            V((gxn, blk, HD), F32),
            V((NCH, requests // 2, cw), F32),
            V((NCH, requests // 2, cw), BF16),
            V((NCH, requests // 2, cw), BF16),
            V((ny, blk, HD), F32),
            V((NCH, ny - 1, blk, cw), BF16),
            V((NCH, ny - 1, blk, cw), BF16),
            V((ny, blk, HD), F32),
            V((ny, blk, HD), F32),
            V((blk, 1), F32),
            V((rl, HD), F32),
            V((rl, HD), F32),
            V((rl, ctx + PAD), F32),
            V((NCH, gyn, rl, cw), BF16),
            V((gyn, NCH, rl, cw), BF16),
            V((rl, hl, HD), F32),
            V((rl, hl, HD), F32),
            V((gyn, rl, hl * HD), BF16),
            V((gxn, gyn, rl, hl * HD), BF16),
            V((requests, HD), F32),
            V((gyn, zblk, hl * HD), BF16),
            V((NOUT, gyn - 1, zblk, ow), BF16),
            V((NOUT, gyn // 2, zblk, ow), BF16),
            V((NOUT, gyn // 2, gyn // 2 - 1, zblk, ow), BF16),
            V((NOUT, zblk, ow), F32),
            V((NOUT, gyn // 2, zblk, ow), F32),
            dma((NCH + 1,)), dma((NOUT,)), dma((2,)),
            dma((NCH + 1,)), dma((NCH + 1,)),
            dma((NCH + 1, ny)), dma((NCH + 1, ny)),
            dma((NCH, gyn)), dma((gyn, NCH)),
            dma((gyn,)), dma((gyn,)),
            dma((ny, gyn)), dma((ny, gyn)),
            dma((ny, gyn)), dma((ny, gyn)),
            dma((NOUT, gyn)), dma((NOUT, gyn // 2)), dma((NOUT, gyn // 2, gyn // 2 - 1)),
        ],
        compiler_params=pltpu.CompilerParams(
            collective_id=0, has_side_effects=True, vmem_limit_bytes=60 * 1024 * 1024
        ),
        cost_estimate=pl.CostEstimate(
            flops=2 * requests * dl * cols, bytes_accessed=2 * dl * cols, transcendentals=0
        ),
    )(
        hidden, cache_row[None, :], ctx_len[None, :],
        w_query, w_key, w_value, w_output, k_cache, v_cache,
    )


def solution(mesh):
    placed = (
        P("groups", "gx"),
        P("groups"),
        P("groups"),
        P("gx", "gy"),
        P("gx", "gy"),
        P("gx", "gy"),
        P("gy", "gx"),
        P(("groups", "gx", "gy"), None, None),
        P(("groups", "gx", "gy"), None, None),
    )
    return jax.shard_map(
        functools.partial(body, mesh.shape["gx"], mesh.shape["gy"]),
        mesh=mesh, in_specs=placed, out_specs=P(("groups", "gy"), "gx"), check_vma=False,
    )
```

```python
import functools
import math

import jax
import jax.numpy as jnp
from jax import lax
from jax.experimental import pallas as pl
from jax.experimental.pallas import tpu as pltpu
from jax.sharding import PartitionSpec as P

D = 8192
H = 64
KVH = 8
HD = 128
EPS = 1e-05
THETA = 500000.0
MESH = pl.DeviceIdType.MESH
F32 = jnp.float32
BF16 = jnp.bfloat16
NCH = 5
NOUT = 4
AHEAD = 5
PAD = 16


def kernel(
    gxn, gyn,
    hidden, crow, clen,
    w_query, w_key, w_value, w_output, k_cache, v_cache,
    out,
    wbuf, wobuf, kbuf, vbuf, ordered, sq, own, xsend, xrecv, sqrecv, ysend, yrecv,
    sqysend, sqyrecv, inv, cos2, sin2, bias, fin, qrecv, qs, os, asend, gath, row_of, perm,
    fsend, frecv, mrecv, facc, fkeep,
    w_sem, wo_sem, kv_sem, xs, xr, ys, yr, qsem, qr, asem, ar, es, er, cs, cr, fs, fr, ms,
):
    gx = lax.axis_index("gx")
    gy = lax.axis_index("gy")
    ny = gxn // 2
    y = gx // 2
    core = gx % 2
    partner = y * 2 + (1 - core)
    ctx = k_cache.shape[1]
    rl = k_cache.shape[0]
    blk = ordered.shape[1]
    requests = blk * gxn
    hl = H // gyn
    kvl = KVH // gyn
    group = H // KVH
    cw = wbuf.shape[2]
    half = cw // 2
    ow = wobuf.shape[2]

    def ypeer(j):
        return lax.rem(y + j, ny)

    def zpeer(k):
        return lax.rem(gy + k, gyn)

    w_copies = [
        [pltpu.make_async_copy(w_query.at[:, pl.ds(c * cw, cw)], wbuf.at[c], w_sem.at[c])]
        for c in range(NCH - 1)
    ]
    w_copies.append([
        pltpu.make_async_copy(w_key, wbuf.at[NCH - 1, :, pl.ds(0, half)], w_sem.at[NCH - 1]),
        pltpu.make_async_copy(w_value, wbuf.at[NCH - 1, :, pl.ds(half, half)], w_sem.at[NCH]),
    ])
    order = [NCH - 1] + list(range(NCH - 1))
    for c in order:
        for copy in w_copies[c]:
            copy.start()
    kv_copies = [
        pltpu.make_async_copy(k_cache, kbuf.at[:, pl.ds(0, ctx), :], kv_sem.at[0]),
        pltpu.make_async_copy(v_cache, vbuf.at[:, pl.ds(0, ctx), :], kv_sem.at[1]),
    ]
    wo_copies = [
        pltpu.make_async_copy(w_output.at[:, pl.ds(n * ow, ow)], wobuf.at[n], wo_sem.at[n])
        for n in range(NOUT)
    ]

    barrier = pltpu.get_barrier_semaphore()
    pl.semaphore_signal(barrier, inc=1, device_id={"gx": partner}, device_id_type=MESH)
    for j in range(1, ny):
        pl.semaphore_signal(
            barrier, inc=1, device_id={"gx": ypeer(j) * 2 + core}, device_id_type=MESH
        )
    for k in range(1, gyn):
        pl.semaphore_signal(barrier, inc=1, device_id={"gy": zpeer(k)}, device_id_type=MESH)

    def reorder(b, carry):
        parity = jnp.where(b < ny, 1 - core, core)
        source = lax.rem(y + lax.rem(b, ny), ny) * 2 + parity
        wanted = lax.broadcasted_iota(jnp.int32, (blk, requests), 0) + source * blk
        chosen = jnp.where(crow[...] == wanted, 1.0, 0.0).astype(BF16)
        rows = jnp.dot(chosen, hidden[...], preferred_element_type=F32)
        ordered[b] = rows.astype(BF16)
        sq[b] = jnp.broadcast_to(jnp.sum(rows * rows, axis=1, keepdims=True), (blk, HD))
        return carry

    for copy in kv_copies + wo_copies:
        copy.start()
    lax.fori_loop(0, gxn, reorder, 0)

    def remote(src, dst, send, recv, **where):
        return pltpu.make_async_remote_copy(
            src_ref=src, dst_ref=dst, send_sem=send, recv_sem=recv,
            device_id=where, device_id_type=MESH,
        )

    def x_copy(c):
        return remote(xsend.at[c], xrecv.at[c], xs.at[c], xr.at[c], gx=partner)

    def y_copy(c, j):
        return remote(
            ysend.at[c, j - 1], yrecv.at[c, j - 1], ys.at[c, j], yr.at[c, j], gx=ypeer(j) * 2 + core
        )

    sq_x = remote(sq.at[pl.ds(0, ny)], sqrecv, xs.at[NCH], xr.at[NCH], gx=partner)

    def sq_y(j):
        return remote(
            sqysend.at[j], sqyrecv.at[j], ys.at[NCH, j], yr.at[NCH, j], gx=ypeer(j) * 2 + core
        )

    def q_copy(c, k):
        peer = zpeer(k)
        return remote(
            fin.at[c, peer], qrecv.at[gy, c], qsem.at[c, k], qr.at[gy, c], gy=peer
        )

    def product(c):
        for copy in w_copies[c]:
            copy.wait()
        rows = ordered[...].reshape(requests, ordered.shape[2])
        part = jnp.dot(rows, wbuf[c], preferred_element_type=F32)
        xsend[c] = part[: requests // 2].astype(BF16)
        own[c] = part[requests // 2 :]

    def stage2(c):
        x_copy(c).wait_recv()
        for j in range(1, ny):
            rows = pl.ds(j * blk, blk)
            ysend[c, j - 1] = (own[c, rows, :] + xrecv[c, rows, :].astype(F32)).astype(BF16)
            y_copy(c, j).start()
        rows = pl.ds(0, blk)
        own[c, rows, :] = own[c, rows, :] + xrecv[c, rows, :].astype(F32)

    def stage3(c):
        total = own[c, pl.ds(0, blk), :]
        for j in range(1, ny):
            y_copy(c, j).wait_recv()
            total = total + yrecv[c, j - 1].astype(F32)
        scaled = (total * inv[...]).astype(BF16)
        for k in range(gyn):
            fin[c, k] = scaled[k * rl : (k + 1) * rl]
        for k in range(1, gyn):
            q_copy(c, k).start()
        qrecv[gy, c] = fin[c, gy]

    for c in order[:AHEAD]:
        product(c)
    first_row = (gx * gyn + gy) * rl
    wanted = lax.broadcasted_iota(jnp.int32, (rl, requests), 0) + first_row
    lengths = jnp.sum(
        jnp.where(crow[...] == wanted, clen[...].astype(F32), 0.0), axis=1, keepdims=True
    )
    lane = lax.broadcasted_iota(jnp.int32, (1, HD), 1)
    pair = lax.rem(lane, HD // 2).astype(F32)
    angle = lengths * jnp.exp(pair * (-2.0 * math.log(THETA) / HD))
    cos2[...] = jnp.cos(angle)
    sine = jnp.sin(angle)
    sin2[...] = jnp.where(lane < HD // 2, -sine, sine)
    slot = lax.broadcasted_iota(jnp.int32, (rl, ctx + PAD), 1)
    bias[...] = jnp.where(
        (slot == ctx) | ((slot < ctx) & (slot.astype(F32) < lengths)), 0.0, -jnp.inf
    )

    def select(b, carry):
        at = pl.ds(pl.multiple_of(b * HD, HD), HD)
        row_of[at, :] = jnp.broadcast_to(crow[:, at].astype(F32), (HD, HD)).T
        return carry

    lax.fori_loop(0, requests // HD, select, 0)
    pl.semaphore_wait(barrier, 1 + (ny - 1) + (gyn - 1))

    sq_x.start()
    for c in order[:AHEAD]:
        x_copy(c).start()
    for step in range(NCH + 2):
        if AHEAD <= step < NCH:
            product(order[step])
            x_copy(order[step]).start()
        if step == 1:
            sq_x.wait_recv()
            for j in range(1, ny):
                sqysend[j] = sq[ny + j] + sqrecv[j]
                sq_y(j).start()
        if 1 <= step <= NCH:
            stage2(order[step - 1])
        if step == 2:
            total = sq[ny] + sqrecv[0]
            for j in range(1, ny):
                sq_y(j).wait_recv()
                total = total + sqyrecv[j]
            inv[...] = lax.rsqrt(total[:, :1] / D + EPS)
        if step >= 2:
            stage3(order[step - 2])
    for copy in kv_copies:
        copy.wait()

    cosine = cos2[...]
    turn = sin2[...]
    scale = 1.0 / math.sqrt(HD)
    top = lax.broadcasted_iota(jnp.int32, (PAD, HD), 0) == 0
    head = lax.broadcasted_iota(jnp.int32, (hl, HD), 0) // group

    def turned(values):
        values = values.astype(F32)
        return values * cosine + pltpu.roll(values, HD // 2, 1) * turn

    def a_copy(k):
        peer = zpeer(k)
        return remote(asend.at[peer], gath.at[gx, gy], asem.at[k], ar.at[gy], gy=peer)

    def e_copy(row, piece, j):
        return remote(
            gath.at[row, piece], gath.at[row, piece], es.at[j, piece], er.at[row // 2, piece],
            gx=ypeer(j) * 2 + core,
        )

    def c_copy(row, piece):
        return remote(
            gath.at[row, piece], gath.at[row, piece], cs.at[row // 2, piece],
            cr.at[row // 2, piece], gx=partner,
        )

    def attention(k, carry):
        source = zpeer(k)

        @pl.when(k > 0)
        def _():
            for c in order:
                remote(
                    fin.at[c, source], qrecv.at[source, c], qsem.at[c, k], qr.at[source, c],
                    gy=source,
                ).wait_recv()

        for h in range(hl):
            at = h * HD
            q = qrecv[source, at // cw, :, at % cw : at % cw + HD]
            qs[:, h, :] = turned(q).astype(BF16).astype(F32)
        for g in range(kvl):
            key = turned(qrecv[source, NCH - 1, :, g * HD : (g + 1) * HD])
            value = qrecv[source, NCH - 1, :, half + g * HD : half + (g + 1) * HD].astype(F32)
            columns = pl.ds(pl.multiple_of((source * kvl + g) * HD, HD), HD)
            for r in range(rl):
                kbuf[r, pl.ds(ctx, PAD), columns] = jnp.where(
                    top, key[r : r + 1], 0.0
                ).astype(BF16)
                vbuf[r, pl.ds(ctx, PAD), columns] = jnp.where(
                    top, value[r : r + 1], 0.0
                ).astype(BF16)
        columns = pl.ds(pl.multiple_of(source * kvl * HD, kvl * HD), kvl * HD)
        scores = []
        for r in range(rl):
            q = qs[r]
            wide = jnp.concatenate(
                [jnp.where(head == g, q, 0.0) for g in range(kvl)], axis=1
            ).astype(BF16)
            scores.append(
                lax.dot_general(
                    wide, kbuf[r, :, columns], (((1,), (1,)), ((), ())),
                    preferred_element_type=F32,
                ) * scale + bias[pl.ds(r, 1), :]
            )
        for r in range(rl):
            highest = jnp.max(scores[r], axis=1, keepdims=True)
            weights = jnp.exp(scores[r] - highest)
            denominator = jnp.sum(weights, axis=1, keepdims=True)
            wide = jnp.dot(
                weights.astype(BF16), vbuf[r, :, columns], preferred_element_type=F32
            )
            picked = wide[:, :HD]
            for g in range(1, kvl):
                picked = jnp.where(head == g, wide[:, g * HD : (g + 1) * HD], picked)
            os[r] = picked / denominator
        for h in range(hl):
            asend[source, :, h * HD : (h + 1) * HD] = os[:, h, :].astype(BF16)

        @pl.when(k > 0)
        def _():
            a_copy(k).start()

        @pl.when(k == 0)
        def _():
            gath[gx, gy] = asend[gy]
            for j in range(1, ny):
                e_copy(gx, gy, j).start()
            c_copy(gx, gy).start()

        return carry

    lax.fori_loop(0, gyn, attention, 0)

    def zback(k):
        return lax.rem(gy - k + gyn, gyn)

    for k in range(1, gyn):
        piece = zback(k)
        remote(
            asend.at[piece], gath.at[gx, piece], asem.at[k], ar.at[piece], gy=piece
        ).wait_recv()
        for j in range(1, ny):
            e_copy(gx, piece, j).start()
        c_copy(gx, piece).start()
    for k in range(gyn):
        piece = zback(k)
        for j in range(1, ny):
            row = ypeer(j) * 2 + core
            e_copy(row, piece, j).wait_recv()
            c_copy(row, piece).start()
    for k in range(gyn):
        piece = zback(k)
        for j in range(ny):
            c_copy(ypeer(j) * 2 + 1 - core, piece).wait_recv()

    zblk = perm.shape[1]
    nh = gyn // 2
    side = gy // nh
    place = lax.rem(gy, nh)
    middle = jnp.where(side == 0, nh - 1 - place, place)

    def at_place(which, m):
        return jnp.where(which == 0, nh - 1 - m, nh + m)

    def target(t):
        if t < nh:
            return at_place(side, lax.rem(middle + t, nh))
        return at_place(1 - side, t - nh)

    for t in range(gyn):
        rows = pl.ds(pl.multiple_of(target(t) * zblk, zblk), zblk)
        lanes = lax.broadcasted_iota(jnp.int32, (zblk, requests), 1).astype(F32)
        chosen = jnp.where(row_of[rows, :1] == lanes, 1.0, 0.0).astype(BF16)
        perm[t] = jnp.dot(
            chosen, gath[...].reshape(requests, hl * HD), preferred_element_type=F32
        ).astype(BF16)

    def f_copy(n, t):
        if t < nh:
            return remote(
                fsend.at[n, t - 1], frecv.at[n, t], fs.at[n, t], fr.at[n, t], gy=target(t)
            )
        return remote(fsend.at[n, t - 1], frecv.at[n, 0], fs.at[n, t], fr.at[n, 0], gy=target(t))

    def m_copy(n, u, m):
        return remote(
            fsend.at[n, nh + u - 1], mrecv.at[n, u, m - 1], fs.at[n, nh + u], ms.at[n, u, m - 1],
            gy=at_place(side, 0),
        )

    def merge(n):
        @pl.when(middle == 0)
        def _():
            for u in range(nh):
                total = fkeep[n, u]
                for m in range(1, nh):
                    m_copy(n, u, m).wait_recv()
                    total = total + mrecv[n, u, m - 1].astype(F32)
                fsend[n, nh + u - 1] = total.astype(BF16)
                f_copy(n, nh + u).start()

    for n in range(NOUT):
        wo_copies[n].wait()
        rows = perm[...].reshape(requests, hl * HD)
        part = jnp.dot(rows, wobuf[n], preferred_element_type=F32)
        facc[n] = part[:zblk]
        for u in range(nh):
            fkeep[n, u] = part[(nh + u) * zblk : (nh + u + 1) * zblk]

        @pl.when(middle > 0)
        def _():
            for u in range(nh):
                fsend[n, nh + u - 1] = fkeep[n, u].astype(BF16)
                m_copy(n, u, middle).start()

        for t in range(1, nh):
            fsend[n, t - 1] = part[t * zblk : (t + 1) * zblk].astype(BF16)
            f_copy(n, t).start()
        if n > 0:
            merge(n - 1)
    merge(NOUT - 1)
    for n in range(NOUT):
        total = facc[n]
        for t in range(nh):
            f_copy(n, t if t > 0 else nh).wait_recv()
            total = total + frecv[n, t].astype(F32)
        out[:, n * ow : (n + 1) * ow] = total.astype(BF16)

    sq_x.wait_send()
    for j in range(1, ny):
        sq_y(j).wait_send()
    for c in range(NCH):
        x_copy(c).wait_send()
        for j in range(1, ny):
            y_copy(c, j).wait_send()
        for k in range(1, gyn):
            q_copy(c, k).wait_send()
    for k in range(1, gyn):
        a_copy(k).wait_send()
    for k in range(gyn):
        piece = zpeer(k)
        for j in range(1, ny):
            e_copy(gx, piece, j).wait_send()
        for j in range(ny):
            c_copy(ypeer(j) * 2 + core, piece).wait_send()
    for n in range(NOUT):
        for t in range(1, gyn):
            f_copy(n, t).wait_send()


def body(gxn, gyn, hidden, cache_row, ctx_len, w_query, w_key, w_value, w_output, k_cache, v_cache):
    requests = cache_row.shape[0]
    rl, ctx, width = k_cache.shape
    ny = gxn // 2
    blk = requests // gxn
    zblk = requests // gyn
    dl = hidden.shape[1]
    hl = H // gyn
    cols = w_query.shape[1] + w_key.shape[1] + w_value.shape[1]
    cw = cols // NCH
    outw = w_output.shape[1]
    ow = outw // NOUT

    vm = pl.BlockSpec(memory_space=pltpu.VMEM)
    hbm = pl.BlockSpec(memory_space=pl.ANY)
    dma = pltpu.SemaphoreType.DMA
    V = pltpu.VMEM
    return pl.pallas_call(
        functools.partial(kernel, gxn, gyn),
        out_shape=jax.ShapeDtypeStruct((zblk, outw), BF16),
        in_specs=[vm] * 3 + [hbm] * 6,
        out_specs=vm,
        scratch_shapes=[
            V((NCH, dl, cw), BF16),
            V((NOUT, hl * HD, ow), BF16),
            V((rl, ctx + PAD, width), BF16),
            V((rl, ctx + PAD, width), BF16),
            V((gxn, blk, dl), BF16),
            V((gxn, blk, HD), F32),
            V((NCH, requests // 2, cw), F32),
            V((NCH, requests // 2, cw), BF16),
            V((NCH, requests // 2, cw), BF16),
            V((ny, blk, HD), F32),
            V((NCH, ny - 1, blk, cw), BF16),
            V((NCH, ny - 1, blk, cw), BF16),
            V((ny, blk, HD), F32),
            V((ny, blk, HD), F32),
            V((blk, 1), F32),
            V((rl, HD), F32),
            V((rl, HD), F32),
            V((rl, ctx + PAD), F32),
            V((NCH, gyn, rl, cw), BF16),
            V((gyn, NCH, rl, cw), BF16),
            V((rl, hl, HD), F32),
            V((rl, hl, HD), F32),
            V((gyn, rl, hl * HD), BF16),
            V((gxn, gyn, rl, hl * HD), BF16),
            V((requests, HD), F32),
            V((gyn, zblk, hl * HD), BF16),
            V((NOUT, gyn - 1, zblk, ow), BF16),
            V((NOUT, gyn // 2, zblk, ow), BF16),
            V((NOUT, gyn // 2, gyn // 2 - 1, zblk, ow), BF16),
            V((NOUT, zblk, ow), F32),
            V((NOUT, gyn // 2, zblk, ow), F32),
            dma((NCH + 1,)), dma((NOUT,)), dma((2,)),
            dma((NCH + 1,)), dma((NCH + 1,)),
            dma((NCH + 1, ny)), dma((NCH + 1, ny)),
            dma((NCH, gyn)), dma((gyn, NCH)),
            dma((gyn,)), dma((gyn,)),
            dma((ny, gyn)), dma((ny, gyn)),
            dma((ny, gyn)), dma((ny, gyn)),
            dma((NOUT, gyn)), dma((NOUT, gyn // 2)), dma((NOUT, gyn // 2, gyn // 2 - 1)),
        ],
        compiler_params=pltpu.CompilerParams(
            collective_id=0, has_side_effects=True, vmem_limit_bytes=60 * 1024 * 1024
        ),
        cost_estimate=pl.CostEstimate(
            flops=2 * requests * dl * cols, bytes_accessed=2 * dl * cols, transcendentals=0
        ),
    )(
        hidden, cache_row[None, :], ctx_len[None, :],
        w_query, w_key, w_value, w_output, k_cache, v_cache,
    )


def solution(mesh):
    placed = (
        P("groups", "gx"),
        P("groups"),
        P("groups"),
        P("gx", "gy"),
        P("gx", "gy"),
        P("gx", "gy"),
        P("gy", "gx"),
        P(("groups", "gx", "gy"), None, None),
        P(("groups", "gx", "gy"), None, None),
    )
    return jax.shard_map(
        functools.partial(body, mesh.shape["gx"], mesh.shape["gy"]),
        mesh=mesh, in_specs=placed, out_specs=P(("groups", "gy"), "gx"), check_vma=False,
    )
```
